32 devices in a mesh: freq: 4 (over y, x), row: 4 (over z), col: 2 (over core).
Axes of the slice: x: 2, y: 2, z: 4, core: 2. Of those that a mesh axis runs over, the one named last changes fastest.
Arguments:
- pair_block: bfloat16 [192, 8192], P('freq', 'row'), may hold values from -6 to 6
- screened: bfloat16 [16, 8192, 8192], P('freq', 'row', 'col'), may hold values from -0.0625 to 0.0625
- pair_gaps: float32 [192], replicated, may hold values from 0.5 to 4
- omega_values: float32 [16], replicated, may hold values from 0.25 to 8
- quad_weight: float32 [16], replicated, may hold values from 0.2 to 1
- freq_slot: int32 [16], replicated, may hold values from 0 to 15, each once
- block_list: int32 [16], replicated, may hold values from 0 to 15, each once
Outputs:
- gamma: float32 [192, 8192], P(('freq', 'row'), 'col')
The draws below stay inside these ranges and needn't reach their ends.
Inputs may be any that keep to these rules, and one draw needn't show every extreme that they name: `freq_slot`: a permutation of the frequencies. `block_list`: a permutation of the blocks.
All inputs are finite; a program needn't handle non-finite values.
Results may differ from the reference program's by a relative error of at most 0.0003.
Values may be sent and summed in bfloat16 or wider, within the bound.
No kernel may reach another device: no remote copies, remote signals or barrier semaphores. Data moves between devices by JAX's collectives and lax.ppermute only.
A program may use at most 128 MiB of HBM per device.

```python
import math
import jax
import jax.numpy as jnp
from jax import lax

NAUX = 8192
PAIRS = 192
NFREQ = 16
NBLK = 16


def with_spikes(drawn, rng, source, target, blocks, factor):
    owner, partner = [(jnp.arange(drawn.shape[position]) // (drawn.shape[position] // blocks)).reshape([-1 if axis == position else 1 for axis in range(drawn.ndim)]) for position in (source, target)]
    chosen = jax.random.permutation(rng, blocks)[partner]
    strong = (owner == chosen) | (owner == (partner + blocks // 2) % blocks)
    return jnp.where(strong, factor * drawn, drawn)


def level_of(rng, dims, shards, low, top_value):
    def one(position, blocks):
        draws = jax.random.uniform(jax.random.fold_in(jax.random.fold_in(rng, 6), position), (blocks,), jnp.float32, low / len(shards), top_value / len(shards))
        return jnp.repeat(jnp.exp(draws), dims[position] // blocks).reshape((-1,) + (1,) * (len(dims) - position - 1))

    gain = one(*shards[0])
    for cut in shards[1:]:
        gain = gain * one(*cut)
    return gain


def centred(rng, dims, spread, limit, shards=(), held_as=jnp.bfloat16):
    array = spread * jax.random.normal(rng, dims, jnp.float32)
    if shards:
        array = array * level_of(rng, dims, shards, -0.22, 0.18)
    return jnp.clip(array, -limit, limit).astype(held_as)


def bell_draw_with(rng, shape, deviation, bound, shards, heavy, kind=jnp.bfloat16):
    values = deviation * jax.random.normal(rng, shape, jnp.float32)
    if shards:
        values = values * level_of(rng, shape, shards, -0.22, 0.18)
    return jnp.clip(with_spikes(values, jax.random.fold_in(rng, 3), *heavy), -bound, bound).astype(kind)


def setup_inputs(seed: int = 0) -> dict:
    seeds = jax.random.split(jax.random.key(seed), 8)
    pair_block = bell_draw_with(seeds[0], (PAIRS, NAUX), 1.0, 6.0, ((0, 4), (1, 4)), (1, 0, 4, 2.0))
    screened = centred(seeds[1], (NFREQ, NAUX, NAUX), NAUX ** -0.5, 0.0625, ((0, 4), (1, 4), (2, 2)))
    pair_gaps = jnp.clip(jnp.exp(jax.random.uniform(seeds[2], (PAIRS,), jnp.float32, math.log(0.5), math.log(4.0))), 0.5, 4.0)
    omega_values = jnp.clip(jnp.exp(jax.random.uniform(seeds[3], (NFREQ,), jnp.float32, math.log(0.25), math.log(8.0))), 0.25, 8.0)
    quad_weight = jnp.clip(jnp.exp(jax.random.uniform(seeds[4], (NFREQ,), jnp.float32, math.log(0.2), math.log(1.0))), 0.2, 1.0)
    freq_slot = jax.random.permutation(seeds[5], NFREQ).astype(jnp.int32)
    block_list = jax.random.permutation(seeds[6], NBLK).astype(jnp.int32)
    return {"pair_block": pair_block, "screened": screened, "pair_gaps": pair_gaps, "omega_values": omega_values, "quad_weight": quad_weight, "freq_slot": freq_slot, "block_list": block_list}


def reference(pair_block, screened, pair_gaps, omega_values, quad_weight, freq_slot, block_list):
    blocks_all = block_list.shape[0]
    rows_each = pair_gaps.shape[0] // blocks_all
    matches = block_list[:, None] == jnp.arange(blocks_all, dtype=jnp.int32)[None, :]
    gap_table = pair_gaps.reshape(blocks_all, rows_each)
    gap_rows = jnp.sum(jnp.where(matches[:, :, None], gap_table[None, :, :], 0.0), axis=1).reshape(-1)
    slots_all = freq_slot.shape[0]
    slot_match = freq_slot[:, None] == jnp.arange(slots_all, dtype=jnp.int32)[None, :]
    omega_slot = jnp.sum(jnp.where(slot_match, omega_values[None, :], 0.0), axis=1)
    weight_slot = jnp.sum(jnp.where(slot_match, quad_weight[None, :], 0.0), axis=1)
    factor = weight_slot[:, None] * 2.0 * gap_rows[None, :] / (gap_rows[None, :] ** 2 + omega_slot[:, None] ** 2)

    def add_slot(running, inputs):
        matrix, scaled = inputs
        product = jnp.dot(pair_block, matrix, preferred_element_type=jnp.float32)
        return running + scaled[:, None] * product, None

    initial = jnp.zeros((PAIRS, NAUX), jnp.float32)
    result, _ = lax.scan(add_slot, initial, (screened, factor))
    return result
```

```python
import functools
import math

import jax
import jax.numpy as jnp
from jax import lax
from jax.experimental import pallas as pl
from jax.experimental.pallas import tpu as pltpu
from jax.sharding import PartitionSpec as P

LANES = 128
TOP = 32700.0
STEPS = 4.0 / math.log(2.0)
VMEM = pl.BlockSpec(memory_space=pltpu.VMEM)
ANY = pl.BlockSpec(memory_space=pl.ANY)


def peer(i, k, n):
    return i ^ k if n & (n - 1) == 0 else (i + k) % n


def send(array, axis, k, n):
    return lax.ppermute(array, axis, [(i, peer(i, k, n)) for i in range(n)])


def fetch(array, axis, k, n):
    return lax.ppermute(array, axis, [(peer(i, k, n), i) for i in range(n)])


def level(high):
    return jnp.ceil(jnp.log(jnp.maximum(high, 1e-30)) * STEPS)


def encode(x, out_ref, rows):
    width = x.shape[1]
    steps = level(jnp.max(jnp.abs(x), axis=1, keepdims=True))
    y = x * (TOP * TOP * jnp.exp(steps * (-1.0 / STEPS)))
    code = jnp.round(y * lax.rsqrt(jnp.abs(y) + 1e-20))
    out_ref[:rows, :width] = code.astype(jnp.int32).astype(jnp.int16)
    out_ref[:rows, width:] = jnp.broadcast_to(steps, (x.shape[0], LANES)).astype(jnp.int32).astype(jnp.int16)


def decode(ref, rows):
    width = ref.shape[1] - LANES
    code = ref[:, :width].astype(jnp.int32).astype(jnp.float32)
    steps = ref[:, width:].astype(jnp.int32).astype(jnp.float32)[:, :1]
    return (code * jnp.abs(code) * (jnp.exp(steps * (1.0 / STEPS)) * (1.0 / (TOP * TOP))))[:rows]


def chunk_kernel(groups, start, tn, ring, *refs):
    b_refs, (fac_ref, w_ref), rest = refs[:groups], refs[groups : groups + 2], refs[groups + 2 :]
    own_ref, msg_refs, (all_rows, acc, buf, sem) = rest[0], rest[1:groups], rest[groups:]
    members = w_ref.shape[0]
    rows, width = own_ref.shape
    pieces = members * (width // tn)
    ring = min(ring, pieces)

    def copy(i, slot):
        column = pl.multiple_of(start + lax.div(i, members) * tn, tn)
        return pltpu.make_async_copy(
            w_ref.at[lax.rem(i, members), :, pl.ds(column, tn)], buf.at[slot], sem.at[slot]
        )

    for i in range(ring):
        copy(i, i).start()
    for k in range(groups):
        all_rows[k * rows : (k + 1) * rows, :] = b_refs[k][...]

    def piece(i, carry):
        slot, member = lax.rem(i, ring), lax.rem(i, members)
        copy(i, slot).wait()
        product = jnp.dot(all_rows[...], buf[slot], preferred_element_type=jnp.float32)
        scaled = product * jnp.tile(fac_ref[member], (1, tn // LANES))
        columns = pl.ds(pl.multiple_of(lax.div(i, members) * tn, tn), tn)

        @pl.when(member == 0)
        def _():
            acc[:, columns] = scaled

        @pl.when(member > 0)
        def _():
            acc[:, columns] += scaled

        @pl.when(i + ring < pieces)
        def _():
            copy(i + ring, slot).start()

        return carry

    lax.fori_loop(0, pieces, piece, 0)
    own_ref[...] = acc[:rows, :]
    for k in range(1, groups):
        encode(acc[k * rows : (k + 1) * rows, :], msg_refs[k - 1], rows)


def chunk(blocks, factor, screened, start, width, tn):
    groups, (rows, depth) = len(blocks), blocks[0].shape
    members = screened.shape[0]
    ring = 6
    outs = [jax.ShapeDtypeStruct((rows, width), jnp.float32)]
    outs += [jax.ShapeDtypeStruct((rows, width + LANES), jnp.int16)] * (groups - 1)
    return pl.pallas_call(
        functools.partial(chunk_kernel, groups, start, tn, ring),
        in_specs=[VMEM] * (groups + 1) + [ANY],
        out_specs=[VMEM] * groups,
        out_shape=outs,
        scratch_shapes=[
            pltpu.VMEM((groups * rows, depth), jnp.bfloat16),
            pltpu.VMEM((groups * rows, width), jnp.float32),
            pltpu.VMEM((ring, depth, tn), jnp.bfloat16),
            pltpu.SemaphoreType.DMA((ring,)),
        ],
        compiler_params=pltpu.CompilerParams(vmem_limit_bytes=40 << 20),
        cost_estimate=pl.CostEstimate(
            flops=2 * groups * rows * depth * width * members,
            bytes_accessed=2 * members * depth * width,
            transcendentals=0,
        ),
        name="weighted_products",
    )(*blocks, factor, screened)


def middle_kernel(groups, members, each, *refs):
    own_ref, got_refs, (mine_ref, *out_refs), total = refs[0], refs[1:groups], refs[groups:-1], refs[-1]
    rows = own_ref.shape[0]
    x = own_ref[...]
    for ref in got_refs:
        x = x + decode(ref, rows)
    total[...] = x
    me = lax.axis_index("row")
    for target in range(members):
        for k in range(members):

            @pl.when(peer(me, k, members) == target)
            def _():
                part = total[target * each : (target + 1) * each, :]
                if k == 0:
                    mine_ref[...] = part
                else:
                    encode(part, out_refs[k - 1], each)


def middle(own, got, members):
    rows, width = own.shape
    each = rows // members
    padded = -(-each // 16) * 16
    outs = [jax.ShapeDtypeStruct((each, width), jnp.float32)]
    outs += [jax.ShapeDtypeStruct((padded, width + LANES), jnp.int16)] * (members - 1)
    return pl.pallas_call(
        functools.partial(middle_kernel, len(got) + 1, members, each),
        in_specs=[VMEM] * (len(got) + 1),
        out_specs=[VMEM] * members,
        out_shape=outs,
        scratch_shapes=[pltpu.VMEM((rows, width), jnp.float32)],
        compiler_params=pltpu.CompilerParams(vmem_limit_bytes=24 << 20),
        name="frequency_sums",
    )(own, *got)


def last_kernel(widths, members, *refs):
    out_ref = refs[-1]
    rows, start = out_ref.shape[0], 0
    for c, width in enumerate(widths):
        mine_ref, *got_refs = refs[c * members : (c + 1) * members]
        x = mine_ref[...]
        for ref in got_refs:
            x = x + decode(ref, rows)
        out_ref[:, start : start + width] = x
        start += width


def last(parts, widths, members):
    rows = parts[0].shape[0]
    return pl.pallas_call(
        functools.partial(last_kernel, widths, members),
        in_specs=[VMEM] * len(parts),
        out_specs=VMEM,
        out_shape=jax.ShapeDtypeStruct((rows, sum(widths)), jnp.float32),
        compiler_params=pltpu.CompilerParams(vmem_limit_bytes=24 << 20),
        name="row_sums",
    )(*parts)


def factors(screened, pair_gaps, omega_values, quad_weight, freq_slot, block_list, groups):
    me = lax.axis_index("freq")
    blocks_all, slots_all = block_list.shape[0], freq_slot.shape[0]
    per = blocks_all // groups
    places = jnp.concatenate([peer(me, k, groups) * per + jnp.arange(per, dtype=jnp.int32) for k in range(groups)])
    every = jnp.arange(blocks_all, dtype=jnp.int32)
    blocks = jnp.sum(jnp.where(places[:, None] == every[None, :], block_list[None, :], 0), axis=1)
    gap_table = pair_gaps.reshape(blocks_all, -1)
    gap_rows = jnp.sum(jnp.where((blocks[:, None] == every[None, :])[:, :, None], gap_table[None, :, :], 0.0), axis=1)
    gap_rows = gap_rows.reshape(-1)
    freq_dev = screened.shape[0]
    slots = lax.dynamic_slice_in_dim(freq_slot, me * freq_dev, freq_dev)
    match = slots[:, None] == jnp.arange(slots_all, dtype=jnp.int32)[None, :]
    omega = jnp.sum(jnp.where(match, omega_values[None, :], 0.0), axis=1)[:, None]
    weight = jnp.sum(jnp.where(match, quad_weight[None, :], 0.0), axis=1)[:, None]
    factor = weight * 2.0 * gap_rows[None, :] / (gap_rows[None, :] ** 2 + omega**2)
    return jnp.broadcast_to(factor[:, :, None], (*factor.shape, LANES))


def split(columns, tn):
    units = columns // tn
    shares = [units // 2, units // 4 + units // 8]
    shares = [s for s in shares if s]
    shares.append(units - sum(shares))
    return [s * tn for s in shares if s]


def local(pair_block, screened, pair_gaps, omega_values, quad_weight, freq_slot, block_list):
    groups, members = lax.axis_size("freq"), lax.axis_size("row")
    columns = screened.shape[2]
    tn = math.gcd(columns, 512)
    blocks = [pair_block] + [fetch(pair_block, "freq", k, groups) for k in range(1, groups)]
    factor = factors(screened, pair_gaps, omega_values, quad_weight, freq_slot, block_list, groups)
    widths, start, parts = split(columns, tn), 0, []
    for width in widths:
        own, *out = chunk(blocks, factor, screened, start, width, tn)
        got = [send(m, "freq", k + 1, groups) for k, m in enumerate(out)]
        mine, *out = middle(own, got, members)
        parts += [mine] + [send(m, "row", k + 1, members) for k, m in enumerate(out)]
        start += width
    return last(parts, widths, members)


def solution(mesh):
    placed = (P("freq", "row"), P("freq", "row", "col"), P(), P(), P(), P(), P())
    return jax.shard_map(
        local, mesh=mesh, in_specs=placed, out_specs=P(("freq", "row"), "col"), check_vma=False
    )
```

```python
import functools
import math

import jax
import jax.numpy as jnp
from jax import lax
from jax.experimental import pallas as pl
from jax.experimental.pallas import tpu as pltpu
from jax.sharding import PartitionSpec as P

LANES = 128
TOP = 32700.0
KEPT = 5
DEPENDS = 1
CUT = 5
STEPS = 4.0 / math.log(2.0)
VMEM = pl.BlockSpec(memory_space=pltpu.VMEM)
ANY = pl.BlockSpec(memory_space=pl.ANY)
HBM = pl.BlockSpec(memory_space=pltpu.HBM)


def peer(i, k, n):
    return i ^ k if n & (n - 1) == 0 else (i + k) % n


def send(array, axis, k, n):
    return lax.ppermute(array, axis, [(i, peer(i, k, n)) for i in range(n)])


def fetch(array, axis, k, n):
    return lax.ppermute(array, axis, [(peer(i, k, n), i) for i in range(n)])


def level(high):
    return jnp.ceil(jnp.log(jnp.maximum(high, 1e-30)) * STEPS)


def codes_of(x):
    steps = level(jnp.max(jnp.abs(x), axis=1, keepdims=True))
    y = x * (TOP * TOP * jnp.exp(steps * (-1.0 / STEPS)))
    return jnp.round(y * lax.rsqrt(jnp.abs(y) + 1e-20)), steps


def short(x):
    return x.astype(jnp.int32).astype(jnp.int16)


def wide(x):
    return x.astype(jnp.int32).astype(jnp.float32)


def values_of(code, steps):
    return code * jnp.abs(code) * (jnp.exp(steps * (1.0 / STEPS)) * (1.0 / (TOP * TOP)))


def encode(x, out_ref):
    rows, width = x.shape
    code, steps = codes_of(x)
    out_ref[:, :width] = short(code)
    out_ref[:, width:] = short(jnp.broadcast_to(steps, (rows, LANES)))


def decode(ref):
    width = ref.shape[1] - LANES
    return values_of(wide(ref[:, :width]), wide(ref[:, width:])[:, :1])


def folded(rows, width):
    if rows == 12 and width % (4 * LANES) == 0:
        return 16, width * 3 // 4 + LANES
    return -(-rows // 16) * 16, width + LANES


def fold(x, out_ref, work):
    rows, width = x.shape
    tall, main = out_ref.shape[0], out_ref.shape[1] - LANES
    code, steps = codes_of(x)
    work[:rows, :main] = code[:, :main]
    if tall > rows and main < width:
        part = width - main
        for i in range(rows):
            below, at = rows + i // 3, i % 3 * part
            work[below : below + 1, at : at + part] = code[i : i + 1, main:]
    elif tall > rows:
        work[rows:tall, :main] = jnp.zeros((tall - rows, main), jnp.float32)
    out_ref[:, :main] = short(work[:tall, :main])
    work[:rows, :LANES] = jnp.broadcast_to(steps, (rows, LANES))
    out_ref[:, main:] = short(work[:tall, :LANES])


def unfold(ref, rows, width, work):
    tall, main = ref.shape[0], ref.shape[1] - LANES
    code = wide(ref[:, :main])
    work[:rows, :main] = code[:rows]
    if main < width:
        part = width - main
        for i in range(rows):
            below, at = rows + i // 3, i % 3 * part
            work[i : i + 1, main:width] = code[below : below + 1, at : at + part]
    return values_of(work[:rows, :width], wide(ref[:, main:])[:rows, :1])


def ahead_kernel(plan, tn, w_ref, *refs):
    small_refs, fac_ref, kept_refs, rest = refs[:5], refs[5], refs[6 : 6 + len(plan)], refs[6 + len(plan) :]
    gap_rows, sem, small_sem, smalls = rest[0], rest[1], rest[2], rest[3:]
    gaps, omegas, weights, slots, blocks = smalls
    members, rows = fac_ref.shape[:2]
    small_copies = [pltpu.make_async_copy(a, b, small_sem.at[i]) for i, (a, b) in enumerate(zip(small_refs, smalls))]
    for c in small_copies:
        c.start()
    copies = []
    for (start, count), kept in zip(plan, kept_refs, strict=True):
        for i in range(count):
            column = start + i // members * tn
            source = w_ref.at[i % members, :, pl.ds(column, tn)]
            copies.append(pltpu.make_async_copy(source, kept.at[i], sem.at[len(copies)]))
            copies[-1].start()
    for c in small_copies:
        c.wait()
    me, groups = lax.axis_index("freq"), lax.axis_size("freq")
    blocks_all = blocks.shape[0]
    per, each = blocks_all // groups, rows // blocks_all
    for k in range(groups):
        place = peer(me, k, groups) * per

        def fill(q, carry):
            first = blocks[place + q] * each
            for i in range(each):
                row = (k * per + q) * each + i
                gap_rows[pl.ds(row, 1), :] = jnp.full((1, LANES), gaps[first + i], jnp.float32)
            return carry

        lax.fori_loop(0, per, fill, 0)
    gap = gap_rows[...]
    for m in range(members):
        slot = slots[me * members + m]
        omega = jnp.full((1, LANES), omegas[slot], jnp.float32)
        weight = jnp.full((1, LANES), weights[slot], jnp.float32)
        fac_ref[m] = weight * 2.0 * gap / (gap * gap + omega * omega)
    for c in copies:
        c.wait()


def ahead(screened, smalls, rows, plan, tn):
    members, depth, _ = screened.shape
    total = sum(count for _, count in plan)
    outs = [jax.ShapeDtypeStruct((members, rows, LANES), jnp.float32)]
    outs += [pltpu.VMEM((count, depth, tn), screened.dtype) for _, count in plan]
    return pl.pallas_call(
        functools.partial(ahead_kernel, plan, tn),
        in_specs=[HBM] * (1 + len(smalls)),
        out_specs=[VMEM] + [ANY] * len(plan),
        out_shape=outs,
        scratch_shapes=[
            pltpu.VMEM((rows, LANES), jnp.float32),
            pltpu.SemaphoreType.DMA((total,)),
            pltpu.SemaphoreType.DMA((len(smalls),)),
        ]
        + [pltpu.SMEM(a.shape, a.dtype) for a in smalls],
        compiler_params=pltpu.CompilerParams(vmem_limit_bytes=2 << 20),
        cost_estimate=pl.CostEstimate(flops=0, bytes_accessed=2 * total * depth * tn, transcendentals=0),
        name="pieces_ahead",
    )(screened, *(pltpu.with_memory_space_constraint(a, pltpu.HBM) for a in smalls))


def chunk_kernel(groups, start, tn, ring, after, *refs):
    b_refs, (fac_ref, kept_ref, w_ref), rest = refs[:groups], refs[groups : groups + 3], refs[groups + 3 + after :]
    own_ref, msg_refs, (all_rows, acc, buf, sem) = rest[0], rest[1:groups], rest[groups:]
    members = w_ref.shape[0]
    rows, width = own_ref.shape
    kept = kept_ref.shape[0]
    pieces = members * (width // tn)
    ring = min(ring, pieces - kept)

    def copy(i, slot):
        column = pl.multiple_of(start + lax.div(i, members) * tn, tn)
        return pltpu.make_async_copy(
            w_ref.at[lax.rem(i, members), :, pl.ds(column, tn)], buf.at[slot], sem.at[slot]
        )

    def add(i, matrix):
        member = lax.rem(i, members)
        product = jnp.dot(all_rows[...], matrix, preferred_element_type=jnp.float32)
        scaled = product * jnp.tile(fac_ref[member], (1, tn // LANES))
        columns = pl.ds(pl.multiple_of(lax.div(i, members) * tn, tn), tn)

        @pl.when(member == 0)
        def _():
            acc[:, columns] = scaled

        @pl.when(member > 0)
        def _():
            acc[:, columns] += scaled

    for i in range(ring):
        copy(kept + i, i).start()
    for k in range(groups):
        all_rows[k * rows : (k + 1) * rows, :] = b_refs[k][...]

    def early(i, carry):
        add(i, kept_ref[i])
        return carry

    def piece(i, carry):
        slot = lax.rem(i - kept, ring)
        copy(i, slot).wait()
        add(i, buf[slot])

        @pl.when(i + ring < pieces)
        def _():
            copy(i + ring, slot).start()

        return carry

    lax.fori_loop(0, kept, early, 0)
    if pieces > kept:
        lax.fori_loop(kept, pieces, piece, 0)
    own_ref[...] = acc[:rows, :]
    for k in range(1, groups):
        encode(acc[k * rows : (k + 1) * rows, :], msg_refs[k - 1])


def chunk(blocks, factor, kept, screened, start, width, tn, after):
    groups, (rows, depth) = len(blocks), blocks[0].shape
    members = screened.shape[0]
    ring = 4
    outs = [jax.ShapeDtypeStruct((rows, width), jnp.float32)]
    outs += [jax.ShapeDtypeStruct((rows, width + LANES), jnp.int16)] * (groups - 1)
    return pl.pallas_call(
        functools.partial(chunk_kernel, groups, start, tn, ring, len(after)),
        in_specs=[VMEM] * (groups + 2) + [ANY] * (1 + len(after)),
        out_specs=[VMEM] * groups,
        out_shape=outs,
        scratch_shapes=[
            pltpu.VMEM((groups * rows, depth), jnp.bfloat16),
            pltpu.VMEM((groups * rows, width), jnp.float32),
            pltpu.VMEM((ring, depth, tn), jnp.bfloat16),
            pltpu.SemaphoreType.DMA((ring,)),
        ],
        compiler_params=pltpu.CompilerParams(vmem_limit_bytes=20 << 20),
        cost_estimate=pl.CostEstimate(
            flops=2 * groups * rows * depth * width * members,
            bytes_accessed=2 * members * depth * width,
            transcendentals=0,
        ),
        name="weighted_products",
    )(*blocks, factor, kept, screened, *after)


def middle_kernel(groups, members, widths, after, *refs):
    chunks = len(widths)
    in_refs, (mine_ref, *out_refs) = refs[: chunks * groups], refs[chunks * groups + after : -3]
    total, picked, work = refs[-3:]
    rows, start = total.shape[0], 0
    each = rows // members
    for c, width in enumerate(widths):
        own_ref, *got_refs = in_refs[c * groups : (c + 1) * groups]
        x = own_ref[...]
        for ref in got_refs:
            x = x + decode(ref)
        total[:, start : start + width] = x
        start += width
    me = lax.axis_index("row")
    for target in range(members):
        for k in range(members):

            @pl.when(peer(me, k, members) == target)
            def _():
                picked[k] = total[target * each : (target + 1) * each, :]

    mine_ref[...] = picked[0]
    for k in range(1, members):
        fold(picked[k], out_refs[k - 1], work)


def middle(chunks, members, after):
    widths = [c[0].shape[1] for c in chunks]
    rows, width = chunks[0][0].shape[0], sum(widths)
    each = rows // members
    shape = folded(each, width)
    outs = [jax.ShapeDtypeStruct((each, width), jnp.float32)]
    outs += [jax.ShapeDtypeStruct(shape, jnp.int16)] * (members - 1)
    flat = [a for c in chunks for a in c]
    return pl.pallas_call(
        functools.partial(middle_kernel, len(chunks[0]), members, widths, len(after)),
        in_specs=[VMEM] * len(flat) + [ANY] * len(after),
        out_specs=[VMEM] * members,
        out_shape=outs,
        scratch_shapes=[
            pltpu.VMEM((rows, width), jnp.float32),
            pltpu.VMEM((members, each, width), jnp.float32),
            pltpu.VMEM(shape, jnp.float32),
        ],
        compiler_params=pltpu.CompilerParams(vmem_limit_bytes=24 << 20),
        name="frequency_sums",
    )(*flat, *after)


def last_kernel(widths, members, *refs):
    out_ref, work = refs[-2:]
    rows, start = out_ref.shape[0], 0
    for c, width in enumerate(widths):
        mine_ref, *got_refs = refs[c * members : (c + 1) * members]
        x = mine_ref[...]
        for ref in got_refs:
            x = x + unfold(ref, rows, width, work)
        out_ref[:, start : start + width] = x
        start += width


def last(parts, widths, members):
    rows = parts[0].shape[0]
    return pl.pallas_call(
        functools.partial(last_kernel, widths, members),
        in_specs=[VMEM] * len(parts),
        out_specs=VMEM,
        out_shape=jax.ShapeDtypeStruct((rows, sum(widths)), jnp.float32),
        scratch_shapes=[pltpu.VMEM((rows, max(widths)), jnp.float32)],
        compiler_params=pltpu.CompilerParams(vmem_limit_bytes=24 << 20),
        name="row_sums",
    )(*parts)


def split(columns, tn):
    units = columns // tn
    cuts = sorted({0, units * CUT // 8, units})
    return [(b - a) * tn for a, b in zip(cuts, cuts[1:])]


def local(pair_block, screened, pair_gaps, omega_values, quad_weight, freq_slot, block_list):
    groups, members = lax.axis_size("freq"), lax.axis_size("row")
    slots, _, columns = screened.shape
    tn = math.gcd(columns, 512)
    blocks = [pair_block] + [fetch(pair_block, "freq", k, groups) for k in range(1, groups)]
    widths = split(columns, tn)
    starts = [sum(widths[:c]) for c in range(len(widths))]
    plan = [(start, min(KEPT, width // tn * slots)) for start, width in zip(starts, widths)]
    smalls = (pair_gaps, omega_values, quad_weight, freq_slot, block_list)
    factor, *kept = ahead(screened, smalls, groups * pair_block.shape[0], plan, tn)
    made, after = [], []
    for c, width in enumerate(widths):
        made.append(chunk(blocks, factor, kept[c], screened, starts[c], width, tn, after))
        after = [made[-1][0]]
    sums = [[own] + [send(m, "freq", k + 1, groups) for k, m in enumerate(out)] for own, *out in made]
    parts, lasts = [], []
    for some in (sums[:-1], sums[-1:]):
        if some:
            mine, *out = middle(some, members, after)
            parts += [mine] + [send(m, "row", k + 1, members) for k, m in enumerate(out)]
            lasts.append(mine.shape[1])
            after = parts[-members + 1 :][:DEPENDS]
    return last(parts, lasts, members)


def solution(mesh):
    placed = (P("freq", "row"), P("freq", "row", "col"), P(), P(), P(), P(), P())
    return jax.shard_map(
        local, mesh=mesh, in_specs=placed, out_specs=P(("freq", "row"), "col"), check_vma=False
    )
```

```python
import functools
import math

import jax
import jax.numpy as jnp
from jax import lax
from jax.experimental import pallas as pl
from jax.experimental.pallas import tpu as pltpu
from jax.sharding import PartitionSpec as P

LANES = 128
TOP = 32700.0
EARLY, NEXT, SPACE = 3, 2, 5
UNIT = 256
SUM_ROWS = 1024
DEPENDS = 1
CUT = 4
STEPS = 4.0 / math.log(2.0)
VMEM = pl.BlockSpec(memory_space=pltpu.VMEM)
ANY = pl.BlockSpec(memory_space=pl.ANY)
HBM = pl.BlockSpec(memory_space=pltpu.HBM)


def peer(i, k, n):
    return i ^ k if n & (n - 1) == 0 else (i + k) % n


def send(array, axis, k, n):
    return lax.ppermute(array, axis, [(i, peer(i, k, n)) for i in range(n)])


def order(n):
    return list(range(n - 1, 0, -1))


def send_all(arrays, axis, n):
    return [send(a, axis, k, n) for k, a in zip(order(n), arrays)]


def fetch(array, axis, k, n):
    return lax.ppermute(array, axis, [(peer(i, k, n), i) for i in range(n)])


def level(high):
    return jnp.ceil(jnp.log(jnp.maximum(high, 1e-30)) * STEPS)


def codes_of(x):
    steps = level(jnp.max(jnp.abs(x), axis=1, keepdims=True))
    y = x * (TOP * TOP * jnp.exp(steps * (-1.0 / STEPS)))
    return jnp.round(y * lax.rsqrt(jnp.abs(y) + 1e-20)), steps


def short(x):
    return x.astype(jnp.int32).astype(jnp.int16)


def wide(x):
    return x.astype(jnp.int32).astype(jnp.float32)


def values_of(code, steps):
    return code * jnp.abs(code) * (jnp.exp(steps * (1.0 / STEPS)) * (1.0 / (TOP * TOP)))


def encode(x, out_ref):
    rows, width = x.shape
    code, steps = codes_of(x)
    out_ref[:, :width] = short(code)
    out_ref[:, width:] = short(jnp.broadcast_to(steps, (rows, LANES)))


def decode(ref):
    width = ref.shape[1] - LANES
    return values_of(wide(ref[:, :width]), wide(ref[:, width:])[:, :1])


def folded(rows, width):
    if rows == 12 and width % (4 * LANES) == 0:
        return 16, width * 3 // 4 + LANES
    return -(-rows // 16) * 16, width + LANES


def fold(x, out_ref, work):
    rows, width = x.shape
    tall, main = out_ref.shape[0], out_ref.shape[1] - LANES
    code, steps = codes_of(x)
    work[:rows, :main] = code[:, :main]
    if tall > rows and main < width:
        part = width - main
        for i in range(rows):
            below, at = rows + i // 3, i % 3 * part
            work[below : below + 1, at : at + part] = code[i : i + 1, main:]
    elif tall > rows:
        work[rows:tall, :main] = jnp.zeros((tall - rows, main), jnp.float32)
    out_ref[:, :main] = short(work[:tall, :main])
    work[:rows, :LANES] = jnp.broadcast_to(steps, (rows, LANES))
    out_ref[:, main:] = short(work[:tall, :LANES])


def unfold(ref, rows, width, work):
    tall, main = ref.shape[0], ref.shape[1] - LANES
    code = wide(ref[:, :main])
    work[:rows, :main] = code[:rows]
    if main < width:
        part = width - main
        for i in range(rows):
            below, at = rows + i // 3, i % 3 * part
            work[i : i + 1, main:width] = code[below : below + 1, at : at + part]
    return values_of(work[:rows, :width], wide(ref[:, main:])[:rows, :1])


def fetch_piece(w_ref, ring_ref, sem, i, tn):
    members, slots = w_ref.shape[0], ring_ref.shape[0]
    if isinstance(i, int):
        member, column, slot = i % members, i // members * tn, i % slots
    else:
        member, column, slot = lax.rem(i, members), pl.multiple_of(lax.div(i, members) * tn, tn), lax.rem(i, slots)
    return pltpu.make_async_copy(w_ref.at[member, :, pl.ds(column, tn)], ring_ref.at[slot], sem.at[slot])


def ahead_kernel(count, tn, w_ref, *refs):
    small_refs, fac_ref, ring_ref, rest = refs[:5], refs[5], refs[6], refs[7:]
    gap_rows, sem, small_sem, smalls = rest[0], rest[1], rest[2], rest[3:]
    gaps, omegas, weights, slots, blocks = smalls
    members, rows = fac_ref.shape[:2]
    small_copies = [pltpu.make_async_copy(a, b, small_sem.at[i]) for i, (a, b) in enumerate(zip(small_refs, smalls))]
    for c in small_copies:
        c.start()
    copies = [fetch_piece(w_ref, ring_ref, sem, i, tn) for i in range(count)]
    for c in copies:
        c.start()
    for c in small_copies:
        c.wait()
    me, groups = lax.axis_index("freq"), lax.axis_size("freq")
    blocks_all = blocks.shape[0]
    per, each = blocks_all // groups, rows // blocks_all
    for k in range(groups):
        place = peer(me, k, groups) * per

        def fill(q, carry):
            first = blocks[place + q] * each
            for i in range(each):
                row = (k * per + q) * each + i
                gap_rows[pl.ds(row, 1), :] = jnp.full((1, LANES), gaps[first + i], jnp.float32)
            return carry

        lax.fori_loop(0, per, fill, 0)
    gap = gap_rows[...]
    for m in range(members):
        slot = slots[me * members + m]
        omega = jnp.full((1, LANES), omegas[slot], jnp.float32)
        weight = jnp.full((1, LANES), weights[slot], jnp.float32)
        fac_ref[m] = weight * 2.0 * gap / (gap * gap + omega * omega)
    for c in copies:
        c.wait()


def ahead(screened, smalls, rows, count, slots, tn):
    members, depth, _ = screened.shape
    return pl.pallas_call(
        functools.partial(ahead_kernel, count, tn),
        in_specs=[HBM] * (1 + len(smalls)),
        out_specs=[VMEM, ANY],
        out_shape=[
            jax.ShapeDtypeStruct((members, rows, LANES), jnp.float32),
            pltpu.VMEM((slots, depth, tn), screened.dtype),
        ],
        scratch_shapes=[
            pltpu.VMEM((rows, LANES), jnp.float32),
            pltpu.SemaphoreType.DMA((slots,)),
            pltpu.SemaphoreType.DMA((len(smalls),)),
        ]
        + [pltpu.SMEM(a.shape, a.dtype) for a in smalls],
        compiler_params=pltpu.CompilerParams(vmem_limit_bytes=2 << 20),
        cost_estimate=pl.CostEstimate(flops=0, bytes_accessed=2 * count * depth * tn, transcendentals=0),
        name="pieces_ahead",
    )(screened, *(pltpu.with_memory_space_constraint(a, pltpu.HBM) for a in smalls))


def chunk_kernel(groups, first_tile, have, want, tn, *refs):
    b_refs, (fac_ref, w_ref, _), rest = refs[:groups], refs[groups : groups + 3], refs[groups + 3 :]
    own_ref, msg_refs, (ring_ref, all_rows, acc, sem) = rest[0], rest[1:groups], rest[groups:]
    (members, depth, _), slots = w_ref.shape, ring_ref.shape[0]
    rows, width = own_ref.shape
    tiles = width // tn
    begin, end = first_tile * members, (first_tile + tiles) * members

    def copy(i):
        return fetch_piece(w_ref, ring_ref, sem, i, tn)

    def add(tile, place, sums):
        units, per = len(sums), tn // UNIT // len(sums)
        order = [(m, c, k) for m in range(members) for c in range(per) for k in range(depth // UNIT)]

        def push(step):
            m, c, k = order[step]
            for u in range(units):
                columns = slice((c * units + u) * UNIT, (c * units + u + 1) * UNIT)
                piece = ring_ref[place + m, k * UNIT : (k + 1) * UNIT, columns]
                pltpu.matmul_push_rhs(piece, step % 2, u)

        def close(m, c):
            for u in range(units):
                product = pltpu.matmul_pop(sums[u][(m * per + c) % len(sums[u])])
                scaled = product * jnp.tile(fac_ref[m], (1, UNIT // LANES))
                column = pl.multiple_of(tile * tn + (c * units + u) * UNIT, UNIT)
                if m == 0:
                    acc[:, pl.ds(column, UNIT)] = scaled
                else:
                    acc[:, pl.ds(column, UNIT)] += scaled

        push(0)
        late = []
        for step, (m, c, k) in enumerate(order):
            if step + 1 < len(order):
                push(step + 1)
            for u in range(units):
                part = all_rows[:, k * UNIT : (k + 1) * UNIT]
                pltpu.matmul_acc_lhs(sums[u][(m * per + c) % len(sums[u])], part, load_staged_rhs=step % 2)
            if late and step >= late[0][0]:
                close(*late.pop(0)[1:])
            if k + 1 == depth // UNIT:
                late.append((step + min(3, depth // UNIT - 1), m, c))
                if len(sums[0]) == 1:
                    close(*late.pop()[1:])
        for _, m, c in late:
            close(m, c)

    for i in range(have, min(want, begin + slots)):
        copy(i).start()
    for k in range(groups):
        all_rows[k * rows : (k + 1) * rows, :] = b_refs[k][...]
    units = 2 if tn % (2 * UNIT) == 0 else 1
    height = groups * rows
    sets = 2 if 2 * height <= SUM_ROWS else 1

    def work(*flat):
        sums = [flat[u * sets : (u + 1) * sets] for u in range(units)]

        def tile(t, carry):
            piece = (first_tile + t) * members
            for m in range(members):

                @pl.when(piece + m >= have)
                def _():
                    copy(piece + m).wait()

            add(t, lax.rem(piece, slots), sums)
            for m in range(members):

                @pl.when(jnp.logical_and(piece + m + slots >= have, piece + m + slots < want))
                def _():
                    copy(piece + m + slots).start()

            return carry

        lax.fori_loop(0, tiles, tile, 0)

    pl.run_scoped(work, *[pltpu.ACC(mxu_id=u)((height, UNIT), jnp.float32) for u in range(units) for _ in range(sets)])
    own_ref[...] = acc[:rows, :]
    for k in range(1, groups):
        encode(acc[k * rows : (k + 1) * rows, :], msg_refs[order(groups).index(k)])
    for i in range(max(have, end), want):
        copy(i).wait()


def chunk(blocks, factor, ring, screened, first_tile, width, have, want, tn):
    groups, (rows, depth) = len(blocks), blocks[0].shape
    members = screened.shape[0]
    outs = [jax.ShapeDtypeStruct((rows, width), jnp.float32)]
    outs += [jax.ShapeDtypeStruct((rows, width + LANES), jnp.int16)] * (groups - 1)
    outs += [pltpu.VMEM(ring.shape, ring.dtype)]
    return pl.pallas_call(
        functools.partial(chunk_kernel, groups, first_tile, have, want, tn),
        in_specs=[VMEM] * (groups + 1) + [HBM, VMEM],
        out_specs=[VMEM] * (groups + 1),
        out_shape=outs,
        input_output_aliases={groups + 2: groups},
        scratch_shapes=[
            pltpu.VMEM((groups * rows, depth), jnp.bfloat16),
            pltpu.VMEM((groups * rows, width), jnp.float32),
            pltpu.SemaphoreType.DMA((ring.shape[0],)),
        ],
        compiler_params=pltpu.CompilerParams(vmem_limit_bytes=8 << 20),
        cost_estimate=pl.CostEstimate(
            flops=2 * groups * rows * depth * width * members,
            bytes_accessed=2 * members * depth * width,
            transcendentals=0,
        ),
        name="weighted_products",
    )(*blocks, factor, screened, ring)


def middle_kernel(groups, members, widths, after, *refs):
    chunks = len(widths)
    in_refs, (mine_ref, *out_refs) = refs[: chunks * groups], refs[chunks * groups + after : -3]
    total, picked, work = refs[-3:]
    rows, start = total.shape[0], 0
    each = rows // members
    for c, width in enumerate(widths):
        own_ref, *got_refs = in_refs[c * groups : (c + 1) * groups]
        x = own_ref[...]
        for ref in got_refs:
            x = x + decode(ref)
        total[:, start : start + width] = x
        start += width
    me = lax.axis_index("row")
    for target in range(members):
        for k in range(members):

            @pl.when(peer(me, k, members) == target)
            def _():
                picked[k] = total[target * each : (target + 1) * each, :]

    mine_ref[...] = picked[0]
    for k, out_ref in zip(order(members), out_refs):
        fold(picked[k], out_ref, work)


def middle(chunks, members, after):
    widths = [c[0].shape[1] for c in chunks]
    rows, width = chunks[0][0].shape[0], sum(widths)
    each = rows // members
    shape = folded(each, width)
    outs = [jax.ShapeDtypeStruct((each, width), jnp.float32)]
    outs += [jax.ShapeDtypeStruct(shape, jnp.int16)] * (members - 1)
    flat = [a for c in chunks for a in c]
    return pl.pallas_call(
        functools.partial(middle_kernel, len(chunks[0]), members, widths, len(after)),
        in_specs=[VMEM] * len(flat) + [ANY] * len(after),
        out_specs=[VMEM] * members,
        out_shape=outs,
        scratch_shapes=[
            pltpu.VMEM((rows, width), jnp.float32),
            pltpu.VMEM((members, each, width), jnp.float32),
            pltpu.VMEM(shape, jnp.float32),
        ],
        compiler_params=pltpu.CompilerParams(vmem_limit_bytes=24 << 20),
        name="frequency_sums",
    )(*flat, *after)


def last_kernel(widths, members, *refs):
    out_ref, work = refs[-2:]
    rows, start = out_ref.shape[0], 0
    for c, width in enumerate(widths):
        mine_ref, *got_refs = refs[c * members : (c + 1) * members]
        x = mine_ref[...]
        for ref in got_refs:
            x = x + unfold(ref, rows, width, work)
        out_ref[:, start : start + width] = x
        start += width


def last(parts, widths, members):
    rows = parts[0].shape[0]
    return pl.pallas_call(
        functools.partial(last_kernel, widths, members),
        in_specs=[VMEM] * len(parts),
        out_specs=VMEM,
        out_shape=jax.ShapeDtypeStruct((rows, sum(widths)), jnp.float32),
        scratch_shapes=[pltpu.VMEM((rows, max(widths)), jnp.float32)],
        compiler_params=pltpu.CompilerParams(vmem_limit_bytes=24 << 20),
        name="row_sums",
    )(*parts)


def split(columns, tn):
    units = columns // tn
    cuts = sorted({0, units * CUT // 8, units})
    return [(b - a) * tn for a, b in zip(cuts, cuts[1:])]


def local(pair_block, screened, pair_gaps, omega_values, quad_weight, freq_slot, block_list):
    groups, members = lax.axis_size("freq"), lax.axis_size("row")
    slots, _, columns = screened.shape
    tn = math.gcd(columns, 512)
    blocks = [pair_block] + [fetch(pair_block, "freq", k, groups) for k in range(1, groups)]
    widths = split(columns, tn)
    smalls = (pair_gaps, omega_values, quad_weight, freq_slot, block_list)
    total = columns // tn * slots
    have = min(EARLY * slots, total)
    factor, ring = ahead(screened, smalls, groups * pair_block.shape[0], have, SPACE * slots, tn)
    made, tile = [], 0
    for width in widths:
        first, tile = tile, tile + width // tn
        want = min((tile + NEXT) * slots, total)
        *out, ring = chunk(blocks, factor, ring, screened, first, width, have, want, tn)
        have = want
        made.append(out)
    after = [made[-1][0]]
    sums = [[own] + send_all(out, "freq", groups) for own, *out in made]
    parts, lasts = [], []
    for some in (sums[:-1], sums[-1:]):
        if some:
            mine, *out = middle(some, members, after)
            parts += [mine] + send_all(out, "row", members)
            lasts.append(mine.shape[1])
            after = parts[-members + 1 :][:DEPENDS]
    return last(parts, lasts, members)


def solution(mesh):
    placed = (P("freq", "row"), P("freq", "row", "col"), P(), P(), P(), P(), P())
    return jax.shard_map(
        local, mesh=mesh, in_specs=placed, out_specs=P(("freq", "row"), "col"), check_vma=False
    )
```
